32 devices in a mesh: dp: 16 (over z, y, x), tensor: 2 (over core).
Axes of the slice: x: 2, y: 2, z: 4, core: 2. Of those that a mesh axis runs over, the one named last changes fastest.
Arguments:
- activations: bfloat16 [20480, 5120], P('dp', 'tensor'), may hold values from -6 to 6
- cotangents: bfloat16 [20480, 1024], P('dp', 'tensor'), as said below
- error_old: bfloat16 [81920, 1024], P(('dp', 'tensor')), may hold values from -3 to 3
- pause_positions: int32 [320], replicated, may hold values from 0 to 1279, as said below
- initial_q: float32 [1024, 32], replicated, may hold values from -6 to 6
Outputs:
- error_new: bfloat16 [81920, 1024], P(('dp', 'tensor'))
- q_factor: float32 [1024, 32], P('tensor')
The draws below stay inside these ranges and needn't reach their ends.
Inputs may be any that keep to these rules, and one draw needn't show every extreme that they name: pause_positions holds 320 different padding positions of a replica's batch, which attention masks out, in no particular order; they are the same for every replica. cotangents lie within 6 / sqrt(1280) in magnitude.
All inputs are finite; a program needn't handle non-finite values.
Results may differ from the reference program's by a relative error of at most 0.002.
Values may be sent and summed in bfloat16 or wider, within the bound.
A program may use at most 64 MiB of HBM per device.

```python
import jax
import jax.numpy as jnp
from jax import lax

D = 5120
KW = 1024
R = 32
TOK_REP = 1280
PAUSES = 320
TOKENS = 20480
N_DP = 16


def mixed_draw(key, row_count, col_count, mixing):
    replicas = TOKENS // TOK_REP
    common = jax.random.normal(jax.random.fold_in(key, 11), (row_count, col_count), jnp.float32)
    private = jax.random.normal(jax.random.fold_in(key, 12), (replicas * row_count, col_count), jnp.float32)
    whole = mixing ** 0.5 * jnp.tile(common, (replicas, 1)) + (1.0 - mixing) ** 0.5 * private
    return jnp.clip(whole, -6.0, 6.0)


def draw_activations(key, part):
    return mixed_draw(jax.random.fold_in(key, 101), TOK_REP, D, 0.8).astype(jnp.bfloat16)


def draw_cotangents(key, part):
    scaled = mixed_draw(jax.random.fold_in(key, 202), TOK_REP, KW, 0.8) * TOK_REP ** (-0.5)
    return scaled.astype(jnp.bfloat16)


def draw_pause_positions(key, part):
    shuffled = jax.random.permutation(jax.random.fold_in(key, 303), TOK_REP)
    return shuffled[:PAUSES].astype(jnp.int32)


def block_scale(own_key, extent, pieces, low, largest):
    level, own = 1.0, jax.random.fold_in(own_key, 6)
    for dim, parts in pieces:
        draws = jnp.exp(jax.random.uniform(jax.random.fold_in(own, dim), (parts,), jnp.float32, low / len(pieces), largest / len(pieces)))
        level = level * jnp.repeat(draws, extent[dim] // parts).reshape([-1 if axis == dim else 1 for axis in range(len(extent))])
    return level


def gaussian(key, dims, spread, most, shards=(), held_as=jnp.bfloat16):
    result = spread * jax.random.normal(key, dims, jnp.float32)
    if shards:
        result = result * block_scale(key, dims, shards, -0.22, 0.18)
    return jnp.clip(result, -most, most).astype(held_as)


def setup_inputs(seed: int = 0) -> dict:
    seeds = jax.random.split(jax.random.key(seed), 6)
    return {
        "activations": draw_activations(jax.random.fold_in(seeds[5], 71), 0),
        "cotangents": draw_cotangents(jax.random.fold_in(seeds[5], 71), 0),
        "error_old": gaussian(seeds[2], (N_DP * D, KW), 0.5, 3.0, ((0, 32),)),
        "pause_positions": draw_pause_positions(jax.random.fold_in(seeds[5], 71), 0),
        "initial_q": gaussian(seeds[4], (KW, R), 1.0, 6.0, (), jnp.float32),
    }


def kept_mask(pause_positions, row_count):
    positions = jnp.arange(row_count, dtype=jnp.int32)
    struck = jnp.any(positions[:, None] == pause_positions[None, :], axis=1)
    return jnp.where(struck, 0, 1).astype(jnp.int32)

def orthonormal(matrix):
    columns = []
    for position in range(matrix.shape[1]):
        column = matrix[:, position]
        for basis in columns:
            column = column - jnp.dot(basis, column, precision=lax.Precision.HIGHEST) * basis
        column = column / jnp.sqrt(jnp.sum(column * column))
        columns.append(column)
    return jnp.stack(columns, axis=1)

def reference(activations, cotangents, error_old, pause_positions, initial_q):
    weights = kept_mask(pause_positions, TOK_REP).astype(jnp.bfloat16)
    contract = (((0,), (0,)), ((), ()))

    def merged_of(replica):
        row_start = (replica * TOK_REP).astype(jnp.int32)
        err_start = (replica * D).astype(jnp.int32)
        feat_rows = lax.dynamic_slice_in_dim(activations, row_start, TOK_REP, 0)
        cot_rows = lax.dynamic_slice_in_dim(cotangents, row_start, TOK_REP, 0) * weights[:, None]
        gradient = lax.dot_general(feat_rows, cot_rows, contract, preferred_element_type=jnp.float32)
        return gradient + lax.dynamic_slice_in_dim(error_old, err_start, D, 0).astype(jnp.float32)

    def accumulate(replica, running):
        return running + merged_of(jnp.asarray(replica).astype(jnp.int32))
    summed = lax.fori_loop(0, N_DP, accumulate, jnp.zeros((D, KW), jnp.float32))
    mean_merged = summed / N_DP
    left_raw = jnp.dot(mean_merged, initial_q, precision=lax.Precision.HIGHEST)
    left_basis = orthonormal(left_raw)
    q_factor = jnp.dot(mean_merged.T, left_basis, precision=lax.Precision.HIGHEST)
    update = jnp.dot(left_basis, q_factor.T, precision=lax.Precision.HIGHEST)

    def fresh_error(replica):
        return (merged_of(replica) - update).astype(jnp.bfloat16)
    errors = lax.map(fresh_error, jnp.arange(N_DP, dtype=jnp.int32))
    return (errors.reshape(N_DP * D, KW), q_factor)
```

```python
import functools
import math

import jax
import jax.numpy as jnp
from jax import lax
from jax.experimental import pallas as pl
from jax.experimental.pallas import tpu as pltpu
from jax.sharding import PartitionSpec as P

F32 = jnp.float32
BF16 = jnp.bfloat16
NN = (((1,), (0,)), ((), ()))
NT = (((1,), (1,)), ((), ()))
TN = (((0,), (0,)), ((), ()))


def mm(a, b, dims):
    return lax.dot_general(a, b, dims, preferred_element_type=F32)


def mm_high(a, b, dims):
    return lax.dot_general(
        a, b, dims, preferred_element_type=F32, precision=lax.Precision.HIGHEST
    )


def pieces(x):
    high = x.astype(BF16)
    rest = x - high.astype(F32)
    middle = rest.astype(BF16)
    low = (rest - middle.astype(F32)).astype(BF16)
    return high, middle, low


def stacked(x):
    return jnp.concatenate(pieces(x), axis=0)


def folded(x):
    n = x.shape[0] // 3
    return x[:n] + x[n : 2 * n] + x[2 * n :]


def inverse_cholesky(gram):
    n = gram.shape[0]
    rows = lax.broadcasted_iota(jnp.int32, (n, n), 0)
    cols = lax.broadcasted_iota(jnp.int32, (n, n), 1)
    left = gram
    right = jnp.where(rows == cols, 1.0, 0.0).astype(F32)
    pivots = jnp.ones((n, n), F32)
    for k in range(n):
        pivot = left[k : k + 1, k : k + 1]
        column = jnp.broadcast_to(left[:, k : k + 1], (n, n))
        pivots = jnp.where(rows == k, jnp.broadcast_to(pivot, (n, n)), pivots)
        factor = jnp.where(rows > k, column / pivot, 0.0)
        left = left - factor * left[k : k + 1, :]
        right = right - factor * right[k : k + 1, :]
    return right / jnp.sqrt(pivots)


def kernel(
    sizes, act_hbm, cot_hbm, err_hbm, pause_ref, q0_ref, out_hbm, q_ref,
    act, cot, err, merged, left_all, left3, parts, sums, sum_in, qall, pcat,
    xa1, ra1, xb1, rb1, gd1, xa2, ra2, xb2, rb2, gd2,
    load_sem, out_sem, t_send, t_recv, s1, r1, s2, r2,
):
    replicas, outer, inner, tens = sizes
    d = lax.axis_index("dp")
    t = lax.axis_index("tensor")
    o, i = d // inner, lax.rem(d, inner)
    row_count, width = act.shape
    kt = cot.shape[2]
    rank = q0_ref.shape[1]

    load_err = pltpu.make_async_copy(err_hbm, err, load_sem.at[0])
    load_cot = pltpu.make_async_copy(cot_hbm, cot.at[t], load_sem.at[1])
    load_act = pltpu.make_async_copy(act_hbm, act, load_sem.at[2])
    load_err.start()
    load_cot.start()
    load_act.start()

    def outer_peer(k):
        return (lax.rem(o + k, outer) * inner + i, t)

    def inner_peer(k):
        return (o * inner + lax.rem(i + k, inner), t)

    def tensor_peer(k):
        return (d, lax.rem(t + k, tens))

    barrier = pltpu.get_barrier_semaphore()
    peers = [outer_peer(k) for k in range(1, outer)]
    peers += [inner_peer(k) for k in range(1, inner)]
    peers += [tensor_peer(k) for k in range(1, tens)]
    for peer in peers:
        pl.semaphore_signal(barrier, inc=1, device_id=peer, device_id_type=pl.DeviceIdType.MESH)
    pl.semaphore_wait(barrier, len(peers))

    sent = []

    def send(src, dst, send_sem, recv_sem, peer):
        copy = pltpu.make_async_remote_copy(
            src_ref=src, dst_ref=dst, send_sem=send_sem, recv_sem=recv_sem,
            device_id=peer, device_id_type=pl.DeviceIdType.MESH,
        )
        copy.start()
        sent.append(copy)
        return copy

    cot_copies = [
        send(cot_hbm, cot.at[t], t_send.at[0, k], t_recv.at[0, k], tensor_peer(k))
        for k in range(1, tens)
    ]

    positions = lax.broadcasted_iota(jnp.int32, (row_count, pause_ref.shape[1]), 0)
    hits = jnp.sum(jnp.where(positions == pause_ref[...], 1.0, 0.0), axis=1, keepdims=True)
    kept = jnp.where(hits == 0.0, 1.0, 0.0).astype(BF16)
    q3 = stacked(q0_ref[...].T)

    load_err.wait()
    from_err = mm(q3, err[...], NT)
    load_cot.wait()
    for copy in cot_copies:
        copy.wait_recv()
    for s in range(tens):
        cot[s] = cot[s] * kept
    tok = mm(q3[:, :kt], cot[0], NT)
    for s in range(1, tens):
        tok = tok + mm(q3[:, s * kt : (s + 1) * kt], cot[s], NT)
    tok3 = stacked(folded(tok))
    load_act.wait()
    own_left = folded(mm(tok3, act[...], NN) + from_err) * (1.0 / replicas)

    tile = math.gcd(width, 256)

    def gradient_tiles(first, last):
        @pl.loop(first, last)
        def _(j):
            here = pl.ds(pl.multiple_of(j * tile, tile), tile)
            block = act[:, here]
            for s in range(tens):
                outs = slice(s * kt, (s + 1) * kt)
                merged[here, outs] = mm(block, cot[s], TN) + err[here, outs].astype(F32)

    def all_reduce(value, bufs, ss, rs, work):
        xa, ra, xb, rb, gd = bufs
        h, span = xa.shape[1], value.shape[1]
        cw = xb.shape[2]
        if span < xa.shape[2]:
            xa[...] = jnp.zeros(xa.shape, F32)
        for p in range(inner):
            xa[p, :, :span] = value[p * h : (p + 1) * h]
        copies = [
            send(xa.at[lax.rem(i + k, inner)], ra.at[k], ss.at[0, k], rs.at[0, k], inner_peer(k))
            for k in range(1, inner)
        ]
        work[0]()
        total = xa[i]
        for k, copy in enumerate(copies, 1):
            copy.wait_recv()
            total = total + ra[k]
        for p in range(outer):
            xb[p] = total[:, p * cw : (p + 1) * cw]
        copies = [
            send(xb.at[lax.rem(o + k, outer)], rb.at[k], ss.at[1, k], rs.at[1, k], outer_peer(k))
            for k in range(1, outer)
        ]
        work[1]()
        total = xb[o]
        for k, copy in enumerate(copies, 1):
            copy.wait_recv()
            total = total + rb[k]
        gd[i, o] = total
        copies = [
            send(gd.at[i, o], gd.at[i, o], ss.at[2, k], rs.at[2, k], outer_peer(k))
            for k in range(1, outer)
        ]
        work[2]()
        for copy in copies:
            copy.wait_recv()
        copies = [
            send(gd.at[i], gd.at[i], ss.at[3, k], rs.at[3, k], inner_peer(k))
            for k in range(1, inner)
        ]
        work[3]()
        for copy in copies:
            copy.wait_recv()
        bands = [
            jnp.concatenate([gd[p, c] for c in range(outer)], axis=1)[:, :span]
            for p in range(inner)
        ]
        return jnp.concatenate(bands, axis=0)

    tiles = width // tile
    marks = [tiles * n // 10 for n in (0, 4, 6, 7, 10)]
    left = all_reduce(
        own_left, (xa1, ra1, xb1, rb1, gd1), s1, r1,
        [functools.partial(gradient_tiles, marks[n], marks[n + 1]) for n in range(4)],
    )
    left_all[t] = left
    left_copies = [
        send(left_all.at[t], left_all.at[t], t_send.at[1, k], t_recv.at[1, k], tensor_peer(k))
        for k in range(1, tens)
    ]

    left3[...] = stacked(left)
    v3 = stacked(folded(mm(left3[...], act[...], NT)))
    s_err = mm(left3[...], err[...], NN)
    for s in range(tens):
        total = s_err[:, s * kt : (s + 1) * kt] + mm(v3, cot[s], NN)
        parts[s] = folded(total) * (1.0 / replicas)
    copies = [
        send(parts.at[lax.rem(t + k, tens)], sum_in.at[k], t_send.at[2, k], t_recv.at[2, k], tensor_peer(k))
        for k in range(1, tens)
    ]

    def first_pass():
        for copy in left_copies:
            copy.wait_recv()
        gram = mm_high(left_all[0], left_all[0], NT)
        for s in range(1, tens):
            gram = gram + mm_high(left_all[s], left_all[s], NT)
        return inverse_cholesky(gram)

    inv1 = first_pass()
    total = parts[t]
    for k, copy in enumerate(copies, 1):
        copy.wait_recv()
        total = total + sum_in[k]

    held = {}

    def second_pass():
        own = mm_high(inv1, left_all[t], NN)
        gram = jnp.zeros((rank, rank), F32)
        for s in range(tens):
            basis = mm_high(inv1, left_all[s], NN)
            gram = gram + mm_high(basis, basis, NT)
        held["inv2"] = inverse_cholesky(gram)
        held["own"] = own

    def own_basis():
        high, middle, _ = pieces(mm_high(held["inv2"], held["own"], NN))
        pcat[...] = jnp.concatenate([high, middle, high], axis=0)

    def nothing():
        pass

    total = all_reduce(
        total, (xa2, ra2, xb2, rb2, gd2), s2, r2, [second_pass, own_basis, nothing, nothing]
    )
    own_q = mm_high(held["inv2"], mm_high(inv1, total, NN), NN)
    qall[t] = own_q
    copies = [
        send(qall.at[t], qall.at[t], t_send.at[3, k], t_recv.at[3, k], tensor_peer(k))
        for k in range(1, tens)
    ]
    q_ref[...] = own_q.T
    for copy in copies:
        copy.wait_recv()

    qcats = []
    for s in range(tens):
        high, middle, _ = pieces(qall[s])
        qcats.append(jnp.concatenate([high, high, middle], axis=0))

    for j in range(tiles):
        here = slice(j * tile, (j + 1) * tile)
        for s in range(tens):
            outs = slice(s * kt, (s + 1) * kt)
            update = mm(pcat[:, here], qcats[s], TN)
            err[here, outs] = (merged[here, outs] - update).astype(BF16)
        pltpu.make_async_copy(err.at[here], out_hbm.at[here], out_sem.at[j]).start()
    for j in range(tiles):
        here = slice(j * tile, (j + 1) * tile)
        pltpu.make_async_copy(err.at[here], out_hbm.at[here], out_sem.at[j]).wait()
    for copy in sent:
        copy.wait_send()


def solution(mesh):
    replicas, tens = mesh.shape["dp"], mesh.shape["tensor"]
    inner = 1
    while inner * inner < replicas or replicas % inner:
        inner += 1
    outer = replicas // inner

    def body(activations, cotangents, error_old, pause_positions, initial_q):
        rows, width = activations.shape
        kt = cotangents.shape[1]
        kw, rank = initial_q.shape
        h = rank // inner
        tile = math.gcd(width, 256)

        def reduce_bufs(span):
            cw = -(-span // (128 * outer)) * 128
            return [
                pltpu.VMEM((inner, h, cw * outer), F32),
                pltpu.VMEM((inner, h, cw * outer), F32),
                pltpu.VMEM((outer, h, cw), F32),
                pltpu.VMEM((outer, h, cw), F32),
                pltpu.VMEM((inner, outer, h, cw), F32),
            ]

        most = max(inner, outer)
        anywhere = pl.BlockSpec(memory_space=pl.ANY)
        vmem = pl.BlockSpec(memory_space=pltpu.VMEM)
        dma = pltpu.SemaphoreType.DMA
        error_new, q = pl.pallas_call(
            functools.partial(kernel, (replicas, outer, inner, tens)),
            out_shape=(
                jax.ShapeDtypeStruct(error_old.shape, BF16),
                jax.ShapeDtypeStruct((kt, rank), F32),
            ),
            in_specs=[anywhere, anywhere, anywhere, vmem, vmem],
            out_specs=(anywhere, vmem),
            scratch_shapes=[
                pltpu.VMEM((rows, width), BF16),
                pltpu.VMEM((tens, rows, kt), BF16),
                pltpu.VMEM((width, kw), BF16),
                pltpu.VMEM((width, kw), F32),
                pltpu.VMEM((tens, rank, width), F32),
                pltpu.VMEM((3 * rank, width), BF16),
                pltpu.VMEM((tens, rank, kt), F32),
                pltpu.VMEM((tens, rank, kt), F32),
                pltpu.VMEM((tens, rank, kt), F32),
                pltpu.VMEM((tens, rank, kt), F32),
                pltpu.VMEM((3 * rank, width), BF16),
                *reduce_bufs(width),
                *reduce_bufs(kt),
                dma((3,)),
                dma((width // tile,)),
                dma((4, tens)),
                dma((4, tens)),
                dma((4, most)),
                dma((4, most)),
                dma((4, most)),
                dma((4, most)),
            ],
            compiler_params=pltpu.CompilerParams(
                collective_id=0, has_side_effects=True, vmem_limit_bytes=56 * 1024 * 1024
            ),
            cost_estimate=pl.CostEstimate(
                flops=2 * rows * width * kw, bytes_accessed=2 * rows * width + 4 * width * kw, transcendentals=0
            ),
        )(activations, cotangents, error_old, pause_positions.reshape(1, -1), initial_q)
        return error_new, q

    return jax.shard_map(
        body,
        mesh=mesh,
        in_specs=(P("dp", "tensor"), P("dp", "tensor"), P(("dp", "tensor"), None), P(), P()),
        out_specs=(P(("dp", "tensor"), None), P("tensor", None)),
        check_vma=False,
    )
```

```python
import functools
import math

import jax
import jax.numpy as jnp
from jax import lax
from jax.experimental import pallas as pl
from jax.experimental.pallas import tpu as pltpu
from jax.sharding import PartitionSpec as P

F32 = jnp.float32
BF16 = jnp.bfloat16
NN = (((1,), (0,)), ((), ()))
NT = (((1,), (1,)), ((), ()))
TN = (((0,), (0,)), ((), ()))


def mm(a, b, dims):
    return lax.dot_general(a, b, dims, preferred_element_type=F32)


def mm_high(a, b, dims):
    return lax.dot_general(
        a, b, dims, preferred_element_type=F32, precision=lax.Precision.HIGHEST
    )


def pieces(x):
    high = x.astype(BF16)
    rest = x - high.astype(F32)
    middle = rest.astype(BF16)
    low = (rest - middle.astype(F32)).astype(BF16)
    return high, middle, low


def stacked(x):
    return jnp.concatenate(pieces(x), axis=0)


def folded(x):
    n = x.shape[0] // 3
    return x[:n] + x[n : 2 * n] + x[2 * n :]


def gram_of(x3):
    g = folded(mm(x3, x3, NT))
    n = g.shape[0]
    return g[:, :n] + g[:, n : 2 * n] + g[:, 2 * n :]


def applied(matrix, x3):
    return folded(mm(stacked(jnp.concatenate([matrix] * 3, axis=1)), x3, NN))


def inverse_cholesky(gram):
    n = gram.shape[0]
    rows = lax.broadcasted_iota(jnp.int32, (n, n), 0)
    cols = lax.broadcasted_iota(jnp.int32, (n, n), 1)
    left = gram
    right = jnp.where(rows == cols, 1.0, 0.0).astype(F32)
    pivots = jnp.ones((n, n), F32)
    for k in range(n):
        column = jnp.broadcast_to(left[:, k : k + 1], (n, n))
        pivots = jnp.where(rows == k, column, pivots)
        scale = 1.0 / column[k : k + 1, :]
        column = jnp.where(rows > k, column, 0.0)
        left_row = left[k : k + 1, :] * scale
        right_row = right[k : k + 1, :] * scale
        left = left - column * left_row
        right = right - column * right_row
    return right / jnp.sqrt(pivots)


def kernel(
    sizes, act_hbm, cot_hbm, err_hbm, pause_ref, q0_ref, merged, pcat, qcat, q_ref,
    act, cot, err, left_all, left3, parts, sum_in, qall,
    xa1, ra1, xb1, rb1, gd1, xa2, ra2, xb2, rb2, gd2,
    load_sem, t_send, t_recv, s1, r1, s2, r2,
):
    replicas, outer, inner, tens = sizes
    d = lax.axis_index("dp")
    t = lax.axis_index("tensor")
    o, i = d // inner, lax.rem(d, inner)
    row_count, width = act.shape
    kt = cot.shape[2]
    rank = q0_ref.shape[0]

    load_err = pltpu.make_async_copy(err_hbm, err, load_sem.at[0])
    load_cot = pltpu.make_async_copy(cot_hbm, cot.at[t], load_sem.at[1])
    load_act = pltpu.make_async_copy(act_hbm, act, load_sem.at[2])
    load_err.start()
    load_cot.start()
    load_act.start()

    def outer_peer(k):
        return (lax.rem(o + k, outer) * inner + i, t)

    def inner_peer(k):
        return (o * inner + lax.rem(i + k, inner), t)

    def tensor_peer(k):
        return (d, lax.rem(t + k, tens))

    barrier = pltpu.get_barrier_semaphore()
    peers = [outer_peer(k) for k in range(1, outer)]
    peers += [inner_peer(k) for k in range(1, inner)]
    peers += [tensor_peer(k) for k in range(1, tens)]
    for peer in peers:
        pl.semaphore_signal(barrier, inc=1, device_id=peer, device_id_type=pl.DeviceIdType.MESH)
    pl.semaphore_wait(barrier, len(peers))

    sent = []

    def send(src, dst, send_sem, recv_sem, peer):
        copy = pltpu.make_async_remote_copy(
            src_ref=src, dst_ref=dst, send_sem=send_sem, recv_sem=recv_sem,
            device_id=peer, device_id_type=pl.DeviceIdType.MESH,
        )
        copy.start()
        sent.append(copy)
        return copy

    cot_copies = [
        send(cot_hbm, cot.at[t], t_send.at[0, k], t_recv.at[0, k], tensor_peer(k))
        for k in range(1, tens)
    ]

    positions = lax.broadcasted_iota(jnp.int32, (row_count, pause_ref.shape[0]), 0)
    hits = jnp.sum(jnp.where(positions == pause_ref[...].reshape(1, -1), 1.0, 0.0), axis=1, keepdims=True)
    kept = jnp.where(hits == 0.0, 1.0, 0.0).astype(BF16)
    q3 = stacked(q0_ref[...])

    load_err.wait()
    from_err = mm(q3, err[...], NT)
    load_cot.wait()
    for copy in cot_copies:
        copy.wait_recv()
    for s in range(tens):
        cot[s] = cot[s] * kept
    tok = mm(q3[:, :kt], cot[0], NT)
    for s in range(1, tens):
        tok = tok + mm(q3[:, s * kt : (s + 1) * kt], cot[s], NT)
    tok3 = stacked(folded(tok))
    load_act.wait()
    own_left = folded(mm(tok3, act[...], NN) + from_err) * (1.0 / replicas)

    tile = math.gcd(width, 256)

    def gradient_tiles(first, last):
        @pl.loop(first, last)
        def _(j):
            here = pl.ds(pl.multiple_of(j * tile, tile), tile)
            block = act[:, here]
            for s in range(tens):
                outs = slice(s * kt, (s + 1) * kt)
                merged[here, outs] = mm(block, cot[s], TN) + err[here, outs].astype(F32)

    def all_reduce(value, bufs, ss, rs, work):
        xa, ra, xb, rb, gd = bufs
        h, span = xa.shape[1], value.shape[1]
        cw = xb.shape[2]
        if span < xa.shape[2]:
            xa[...] = jnp.zeros(xa.shape, F32)
        for p in range(inner):
            xa[p, :, :span] = value[p * h : (p + 1) * h]
        copies = [
            send(xa.at[lax.rem(i + k, inner)], ra.at[k], ss.at[0, k], rs.at[0, k], inner_peer(k))
            for k in range(1, inner)
        ]
        work[0]()
        total = xa[i]
        for k, copy in enumerate(copies, 1):
            copy.wait_recv()
            total = total + ra[k]
        for p in range(outer):
            xb[p] = total[:, p * cw : (p + 1) * cw]
        copies = [
            send(xb.at[lax.rem(o + k, outer)], rb.at[k], ss.at[1, k], rs.at[1, k], outer_peer(k))
            for k in range(1, outer)
        ]
        work[1]()
        total = xb[o]
        for k, copy in enumerate(copies, 1):
            copy.wait_recv()
            total = total + rb[k]
        gd[i, o] = total
        copies = [
            send(gd.at[i, o], gd.at[i, o], ss.at[2, k], rs.at[2, k], outer_peer(k))
            for k in range(1, outer)
        ]
        work[2]()
        for copy in copies:
            copy.wait_recv()
        copies = [
            send(gd.at[i], gd.at[i], ss.at[3, k], rs.at[3, k], inner_peer(k))
            for k in range(1, inner)
        ]
        work[3]()
        for copy in copies:
            copy.wait_recv()
        bands = [
            jnp.concatenate([gd[p, c] for c in range(outer)], axis=1)[:, :span]
            for p in range(inner)
        ]
        return jnp.concatenate(bands, axis=0)

    tiles = width // tile
    marks = [tiles * n // 10 for n in (0, 3, 5, 7, 10)]
    left = all_reduce(
        own_left, (xa1, ra1, xb1, rb1, gd1), s1, r1,
        [functools.partial(gradient_tiles, marks[n], marks[n + 1]) for n in range(4)],
    )
    left_all[t] = left
    left_copies = [
        send(left_all.at[t], left_all.at[t], t_send.at[1, k], t_recv.at[1, k], tensor_peer(k))
        for k in range(1, tens)
    ]

    own3 = stacked(left)
    left3[t] = own3
    v3 = stacked(folded(mm(own3, act[...], NT)))
    for copy in left_copies:
        copy.wait_recv()
    for k in range(1, tens):
        peer = lax.rem(t + k, tens)
        left3[peer] = stacked(left_all[peer])
    gram = gram_of(left3[0])
    for s in range(1, tens):
        gram = gram + gram_of(left3[s])
    inv1 = inverse_cholesky(gram)
    s_err = mm(left3[t], err[...], NN)
    for s in range(tens):
        total = s_err[:, s * kt : (s + 1) * kt] + mm(v3, cot[s], NN)
        parts[s] = folded(total) * (1.0 / replicas)
    copies = [
        send(parts.at[lax.rem(t + k, tens)], sum_in.at[k], t_send.at[2, k], t_recv.at[2, k], tensor_peer(k))
        for k in range(1, tens)
    ]
    held = {}

    def second_gram():
        gram = jnp.zeros((rank, rank), F32)
        for s in range(tens):
            basis3 = stacked(applied(inv1, left3[s]))
            left3[s] = basis3
            gram = gram + gram_of(basis3)
        held["gram"] = gram

    def second_inverse():
        held["inv2"] = inverse_cholesky(held["gram"])
        held["both"] = mm_high(held["inv2"], inv1, NN)

    def own_basis():
        high, middle, _ = pieces(applied(held["inv2"], left3[t]))
        pcat[...] = jnp.concatenate([high, middle, high], axis=0)

    def nothing():
        pass

    second_gram()
    total = parts[t]
    for k, copy in enumerate(copies, 1):
        copy.wait_recv()
        total = total + sum_in[k]
    total = all_reduce(
        total, (xa2, ra2, xb2, rb2, gd2), s2, r2, [second_inverse, own_basis, nothing, nothing]
    )
    own_q = mm_high(held["both"], total, NN)
    qall[t] = own_q
    copies = [
        send(qall.at[t], qall.at[t], t_send.at[3, k], t_recv.at[3, k], tensor_peer(k))
        for k in range(1, tens)
    ]
    q_ref[...] = own_q
    for copy in copies:
        copy.wait_recv()
    for s in range(tens):
        high, middle, _ = pieces(qall[s])
        qcat[s] = jnp.concatenate([high, high, middle], axis=0)
    for copy in sent:
        copy.wait_send()


def update_kernel(tile, merged, pcat, qcat, q_in, out_hbm, q_out, out, sems):
    tens, _, kt = qcat.shape
    copies = []
    for j in range(out.shape[0] // tile):
        here = slice(j * tile, (j + 1) * tile)
        for s in range(tens):
            outs = slice(s * kt, (s + 1) * kt)
            update = mm(pcat[:, here], qcat[s], TN)
            out[here, outs] = (merged[here, outs] - update).astype(BF16)
        copy = pltpu.make_async_copy(out.at[here], out_hbm.at[here], sems.at[j])
        copy.start()
        copies.append(copy)
    q_out[...] = q_in[...]
    for copy in copies:
        copy.wait()


def solution(mesh):
    replicas, tens = mesh.shape["dp"], mesh.shape["tensor"]
    inner = 1
    while inner * inner < replicas or replicas % inner:
        inner += 1
    outer = replicas // inner

    def body(activations, cotangents, error_old, pause_positions, initial_q):
        rows, width = activations.shape
        kt = cotangents.shape[1]
        kw, rank = initial_q.shape
        mib = 1024 * 1024
        h = rank // inner
        tile = math.gcd(width, 256)

        def reduce_bufs(span):
            cw = -(-span // (128 * outer)) * 128
            return [
                pltpu.VMEM((inner, h, cw * outer), F32),
                pltpu.VMEM((inner, h, cw * outer), F32),
                pltpu.VMEM((outer, h, cw), F32),
                pltpu.VMEM((outer, h, cw), F32),
                pltpu.VMEM((inner, outer, h, cw), F32),
            ]

        most = max(inner, outer)
        hbm = pl.BlockSpec(memory_space=pltpu.HBM)
        vmem = pl.BlockSpec(memory_space=pltpu.VMEM)
        dma = pltpu.SemaphoreType.DMA
        merged, pcat, qcat, own_q = pl.pallas_call(
            functools.partial(kernel, (replicas, outer, inner, tens)),
            out_shape=(
                pltpu.VMEM((width, kw), F32),
                pltpu.VMEM((3 * rank, width), BF16),
                pltpu.VMEM((tens, 3 * rank, kt), BF16),
                pltpu.VMEM((rank, kt), F32),
            ),
            in_specs=[hbm, hbm, hbm, vmem, vmem],
            out_specs=(vmem,) * 4,
            scratch_shapes=[
                pltpu.VMEM((rows, width), BF16),
                pltpu.VMEM((tens, rows, kt), BF16),
                pltpu.VMEM((width, kw), BF16),
                pltpu.VMEM((tens, rank, width), F32),
                pltpu.VMEM((tens, 3 * rank, width), BF16),
                pltpu.VMEM((tens, rank, kt), F32),
                pltpu.VMEM((tens, rank, kt), F32),
                pltpu.VMEM((tens, rank, kt), F32),
                *reduce_bufs(width),
                *reduce_bufs(kt),
                dma((3,)),
                dma((4, tens)),
                dma((4, tens)),
                dma((4, most)),
                dma((4, most)),
                dma((4, most)),
                dma((4, most)),
            ],
            compiler_params=pltpu.CompilerParams(
                collective_id=0, has_side_effects=True, vmem_limit_bytes=36 * mib
            ),
            cost_estimate=pl.CostEstimate(
                flops=2 * rows * width * kw, bytes_accessed=2 * rows * width + 4 * width * kw, transcendentals=0
            ),
        )(*(
            pltpu.with_memory_space_constraint(x, pltpu.HBM)
            for x in (activations, cotangents, error_old, pause_positions, initial_q.T)
        ))
        error_new, q = pl.pallas_call(
            functools.partial(update_kernel, tile),
            out_shape=(
                jax.ShapeDtypeStruct(error_old.shape, BF16),
                jax.ShapeDtypeStruct((rank, kt), F32),
            ),
            in_specs=[vmem] * 4,
            out_specs=(hbm, vmem),
            scratch_shapes=[pltpu.VMEM((width, kw), BF16), dma((width // tile,))],
            compiler_params=pltpu.CompilerParams(vmem_limit_bytes=16 * mib),
        )(merged, pcat, qcat, own_q)
        return error_new, q.T

    return jax.shard_map(
        body,
        mesh=mesh,
        in_specs=(P("dp", "tensor"), P("dp", "tensor"), P(("dp", "tensor"), None), P(), P()),
        out_specs=(P(("dp", "tensor"), None), P("tensor", None)),
        check_vma=False,
    )
```

```python
import functools
import math

import jax
import jax.numpy as jnp
from jax import lax
from jax.experimental import pallas as pl
from jax.experimental.pallas import tpu as pltpu
from jax.sharding import PartitionSpec as P

F32 = jnp.float32
BF16 = jnp.bfloat16
NN = (((1,), (0,)), ((), ()))
NT = (((1,), (1,)), ((), ()))
TN = (((0,), (0,)), ((), ()))


def mm(a, b, dims):
    return lax.dot_general(a, b, dims, preferred_element_type=F32)


def mm_high(a, b, dims):
    return lax.dot_general(
        a, b, dims, preferred_element_type=F32, precision=lax.Precision.HIGHEST
    )


def pieces(x):
    high = x.astype(BF16)
    rest = x - high.astype(F32)
    middle = rest.astype(BF16)
    low = (rest - middle.astype(F32)).astype(BF16)
    return high, middle, low


def stacked(x):
    return jnp.concatenate(pieces(x), axis=0)


def folded(x):
    n = x.shape[0] // 3
    return x[:n] + x[n : 2 * n] + x[2 * n :]


def gram_of(x3):
    g = folded(mm(x3, x3, NT))
    n = g.shape[0]
    return g[:, :n] + g[:, n : 2 * n] + g[:, 2 * n :]


def applied(matrix, x3):
    return folded(mm(stacked(jnp.concatenate([matrix] * 3, axis=1)), x3, NN))


def inverse_cholesky(gram):
    n = gram.shape[0]
    rows = lax.broadcasted_iota(jnp.int32, (n, n), 0)
    cols = lax.broadcasted_iota(jnp.int32, (n, n), 1)
    left = gram
    right = jnp.where(rows == cols, 1.0, 0.0).astype(F32)
    pivots = jnp.ones((n, n), F32)
    for k in range(n):
        column = jnp.broadcast_to(left[:, k : k + 1], (n, n))
        pivots = jnp.where(rows == k, column, pivots)
        scale = 1.0 / column[k : k + 1, :]
        column = jnp.where(rows > k, column, 0.0)
        left_row = left[k : k + 1, :] * scale
        right_row = right[k : k + 1, :] * scale
        left = left - column * left_row
        right = right - column * right_row
    return right / jnp.sqrt(pivots)


def kernel(
    sizes, act_hbm, cot_hbm, err_hbm, pause_ref, q0_ref, merged, pcat, qcat, q_ref,
    act, cot, err, left_all, left3, parts, sum_in, qall,
    xa1, ra1, xb1, rb1, gd1, xa2, ra2, xb2, rb2, gd2, xa3, ra3, xb3, rb3, gd3,
    err_sem, act_sem, cot_sem, t_send, t_recv, s1, r1, s2, r2, s3, r3,
):
    replicas, outer, inner, tens, split, direct = sizes
    d = lax.axis_index("dp")
    t = lax.axis_index("tensor")
    o, i = d // inner, lax.rem(d, inner)
    row_count, width = act.shape
    kt = cot.shape[2]
    rank = q0_ref.shape[0]

    loads = err_sem.shape[0]
    load_cot = pltpu.make_async_copy(cot_hbm, cot.at[t], cot_sem.at[0])
    load_cot.start()

    def load(src, dst, sems):
        step = src.shape[0] // loads
        copies = []
        for n in range(loads):
            here = pl.ds(n * step, step)
            copies.append(pltpu.make_async_copy(src.at[here], dst.at[here], sems.at[n]))
        return copies

    load_err = load(err_hbm, err, err_sem)
    load_act = load(act_hbm, act, act_sem)
    for copy in load_err:
        copy.start()

    def outer_peer(k):
        return (lax.rem(o + k, outer) * inner + i, t)

    def inner_peer(k):
        return (o * inner + lax.rem(i + k, inner), t)

    def any_peer(k):
        return (lax.rem(d + k, replicas), t)

    def tensor_peer(k):
        return (d, lax.rem(t + k, tens))

    barrier = pltpu.get_barrier_semaphore()
    if direct:
        peers = [any_peer(k) for k in range(1, replicas)]
    else:
        peers = [outer_peer(k) for k in range(1, outer)]
        peers += [inner_peer(k) for k in range(1, inner)]
    peers += [tensor_peer(k) for k in range(1, tens)]
    for peer in peers:
        pl.semaphore_signal(barrier, inc=1, device_id=peer, device_id_type=pl.DeviceIdType.MESH)
    pl.semaphore_wait(barrier, len(peers))

    sent = []

    def send(src, dst, send_sem, recv_sem, peer):
        copy = pltpu.make_async_remote_copy(
            src_ref=src, dst_ref=dst, send_sem=send_sem, recv_sem=recv_sem,
            device_id=peer, device_id_type=pl.DeviceIdType.MESH,
        )
        copy.start()
        sent.append(copy)
        return copy

    cot_copies = [
        send(cot_hbm, cot.at[t], t_send.at[0, k], t_recv.at[0, k], tensor_peer(k))
        for k in range(1, tens)
    ]

    positions = lax.broadcasted_iota(jnp.int32, (row_count, pause_ref.shape[0]), 0)
    hits = jnp.sum(jnp.where(positions == pause_ref[...].reshape(1, -1), 1.0, 0.0), axis=1, keepdims=True)
    kept = jnp.where(hits == 0.0, 1.0, 0.0).astype(BF16)
    q3 = stacked(q0_ref[...])

    from_err = []
    step = width // loads
    for n, copy in enumerate(load_err):
        copy.wait()
        load_act[n].start()
        from_err.append(mm(q3, err[n * step : (n + 1) * step], NT))
    from_err = jnp.concatenate(from_err, axis=1)
    load_cot.wait()
    for copy in cot_copies:
        copy.wait_recv()
    for s in range(tens):
        cot[s] = cot[s] * kept
    tok = mm(q3[:, :kt], cot[0], NT)
    for s in range(1, tens):
        tok = tok + mm(q3[:, s * kt : (s + 1) * kt], cot[s], NT)
    tok3 = stacked(folded(tok))
    for copy in load_act:
        copy.wait()

    def left_part(first, last):
        whole = mm(tok3, act[:, first:last], NN) + from_err[:, first:last]
        return folded(whole) * (1.0 / replicas)

    tile = math.gcd(width, 256)

    def gradient_tiles(first, last):
        @pl.loop(first, last)
        def _(j):
            here = pl.ds(pl.multiple_of(j * tile, tile), tile)
            block = act[:, here]
            for s in range(tens):
                outs = slice(s * kt, (s + 1) * kt)
                merged[here, outs] = mm(block, cot[s], TN) + err[here, outs].astype(F32)

    def all_reduce(value, bufs, ss, rs, first, second):
        (own1, n1, peer1), (own2, n2, peer2) = first, second
        xa, ra, xb, rb, gd = bufs
        h, span = xa.shape[1], value.shape[1]
        cw = xb.shape[2]
        if span < xa.shape[2]:
            xa[...] = jnp.zeros(xa.shape, F32)
        for p in range(n1):
            xa[p, :, :span] = value[p * h : (p + 1) * h]
        copies = [
            send(xa.at[lax.rem(own1 + k, n1)], ra.at[k], ss.at[0, k], rs.at[0, k], peer1(k))
            for k in range(1, n1)
        ]
        yield
        total = xa[own1]
        for k, copy in enumerate(copies, 1):
            copy.wait_recv()
            total = total + ra[k]
        if n2 > 1:
            for p in range(n2):
                xb[p] = total[:, p * cw : (p + 1) * cw]
            copies = [
                send(xb.at[lax.rem(own2 + k, n2)], rb.at[k], ss.at[1, k], rs.at[1, k], peer2(k))
                for k in range(1, n2)
            ]
            yield
            total = xb[own2]
            for k, copy in enumerate(copies, 1):
                copy.wait_recv()
                total = total + rb[k]
            gd[own1, own2] = total
            copies = [
                send(gd.at[own1, own2], gd.at[own1, own2], ss.at[2, k], rs.at[2, k], peer2(k))
                for k in range(1, n2)
            ]
            yield
            for copy in copies:
                copy.wait_recv()
        else:
            gd[own1, 0] = total
        copies = [
            send(gd.at[own1], gd.at[own1], ss.at[3, k], rs.at[3, k], peer1(k))
            for k in range(1, n1)
        ]
        yield
        for copy in copies:
            copy.wait_recv()
        bands = [
            jnp.concatenate([gd[p, c] for c in range(n2)], axis=1)[:, :span]
            for p in range(n1)
        ]
        yield jnp.concatenate(bands, axis=0)

    by_inner = (i, inner, inner_peer)
    by_outer = (o, outer, outer_peer)
    tiles = width // tile
    marks = [tiles * n // 10 for n in (0, 3, 5, 7, 9)]
    run1 = all_reduce(left_part(0, split), (xa1, ra1, xb1, rb1, gd1), s1, r1, by_outer, by_inner)
    next(run1)
    run2 = all_reduce(left_part(split, width), (xa2, ra2, xb2, rb2, gd2), s2, r2, by_inner, by_outer)
    next(run2)
    for n in range(4):
        gradient_tiles(marks[n], marks[n + 1])
        part2 = next(run2)
        part1 = next(run1)
    left = jnp.concatenate([part1, part2], axis=1)
    left_all[t] = left
    left_copies = [
        send(left_all.at[t], left_all.at[t], t_send.at[1, k], t_recv.at[1, k], tensor_peer(k))
        for k in range(1, tens)
    ]

    own3 = stacked(left)
    left3[t] = own3
    v3 = stacked(folded(mm(own3, act[...], NT)))
    for copy in left_copies:
        copy.wait_recv()
    for k in range(1, tens):
        peer = lax.rem(t + k, tens)
        left3[peer] = stacked(left_all[peer])
    gram = gram_of(left3[0])
    for s in range(1, tens):
        gram = gram + gram_of(left3[s])
    inv1 = inverse_cholesky(gram)
    s_err = mm(left3[t], err[...], NN)
    for s in range(tens):
        total = s_err[:, s * kt : (s + 1) * kt] + mm(v3, cot[s], NN)
        parts[s] = folded(total) * (1.0 / replicas)
    copies = [
        send(parts.at[lax.rem(t + k, tens)], sum_in.at[k], t_send.at[2, k], t_recv.at[2, k], tensor_peer(k))
        for k in range(1, tens)
    ]
    held = {}

    def second_gram():
        gram = jnp.zeros((rank, rank), F32)
        for s in range(tens):
            basis3 = stacked(applied(inv1, left3[s]))
            left3[s] = basis3
            gram = gram + gram_of(basis3)
        held["gram"] = gram

    def second_inverse():
        held["inv2"] = inverse_cholesky(held["gram"])
        held["both"] = mm_high(held["inv2"], inv1, NN)

    def own_basis():
        high, middle, _ = pieces(applied(held["inv2"], left3[t]))
        pcat[...] = jnp.concatenate([high, middle, high], axis=0)

    second_gram()
    total = parts[t]
    for k, copy in enumerate(copies, 1):
        copy.wait_recv()
        total = total + sum_in[k]
    groups = ((d, replicas, any_peer), (0, 1, None)) if direct else (by_inner, by_outer)
    run3 = all_reduce(total, (xa3, ra3, xb3, rb3, gd3), s3, r3, *groups)
    next(run3)
    second_inverse()
    total = next(run3)
    own_basis()
    while total is None:
        total = next(run3)
    own_q = mm_high(held["both"], total, NN)
    qall[t] = own_q
    copies = [
        send(qall.at[t], qall.at[t], t_send.at[3, k], t_recv.at[3, k], tensor_peer(k))
        for k in range(1, tens)
    ]
    q_ref[...] = own_q
    gradient_tiles(marks[4], tiles)
    for copy in copies:
        copy.wait_recv()
    for s in range(tens):
        high, middle, _ = pieces(qall[s])
        qcat[s] = jnp.concatenate([high, high, middle], axis=0)
    for copy in sent:
        copy.wait_send()


def update_kernel(tile, merged, pcat, qcat, q_in, out_hbm, q_out, out, sems):
    tens, _, kt = qcat.shape
    copies = []
    for j in range(out.shape[0] // tile):
        here = slice(j * tile, (j + 1) * tile)
        for s in range(tens):
            outs = slice(s * kt, (s + 1) * kt)
            update = mm(pcat[:, here], qcat[s], TN)
            out[here, outs] = (merged[here, outs] - update).astype(BF16)
        copy = pltpu.make_async_copy(out.at[here], out_hbm.at[here], sems.at[j])
        copy.start()
        copies.append(copy)
    q_out[...] = q_in[...]
    for copy in copies:
        copy.wait()


def solution(mesh):
    replicas, tens = mesh.shape["dp"], mesh.shape["tensor"]
    inner = 1
    while inner * inner < replicas or replicas % inner:
        inner += 1
    outer = replicas // inner

    def body(activations, cotangents, error_old, pause_positions, initial_q):
        rows, width = activations.shape
        kt = cotangents.shape[1]
        kw, rank = initial_q.shape
        mib = 1024 * 1024
        tile = math.gcd(width, 256)
        split = 2 * width // 5 // 128 * 128
        direct = replicas <= min(rank, 16)
        loads = 4 if width % 512 == 0 and rows % 64 == 0 else 1

        def reduce_bufs(span, n1, n2):
            h, cw = rank // n1, -(-span // (128 * n2)) * 128
            return [
                pltpu.VMEM((n1, h, cw * n2), F32),
                pltpu.VMEM((n1, h, cw * n2), F32),
                pltpu.VMEM((n2, h, cw), F32),
                pltpu.VMEM((n2, h, cw), F32),
                pltpu.VMEM((n1, n2, h, cw), F32),
            ]

        most = replicas if direct else max(inner, outer)
        hbm = pl.BlockSpec(memory_space=pltpu.HBM)
        vmem = pl.BlockSpec(memory_space=pltpu.VMEM)
        dma = pltpu.SemaphoreType.DMA
        merged, pcat, qcat, own_q = pl.pallas_call(
            functools.partial(kernel, (replicas, outer, inner, tens, split, direct)),
            out_shape=(
                pltpu.VMEM((width, kw), F32),
                pltpu.VMEM((3 * rank, width), BF16),
                pltpu.VMEM((tens, 3 * rank, kt), BF16),
                pltpu.VMEM((rank, kt), F32),
            ),
            in_specs=[hbm, hbm, hbm, vmem, vmem],
            out_specs=(vmem,) * 4,
            scratch_shapes=[
                pltpu.VMEM((rows, width), BF16),
                pltpu.VMEM((tens, rows, kt), BF16),
                pltpu.VMEM((width, kw), BF16),
                pltpu.VMEM((tens, rank, width), F32),
                pltpu.VMEM((tens, 3 * rank, width), BF16),
                pltpu.VMEM((tens, rank, kt), F32),
                pltpu.VMEM((tens, rank, kt), F32),
                pltpu.VMEM((tens, rank, kt), F32),
                *reduce_bufs(split, outer, inner),
                *reduce_bufs(width - split, inner, outer),
                *(reduce_bufs(kt, replicas, 1) if direct else reduce_bufs(kt, inner, outer)),
                dma((loads,)),
                dma((loads,)),
                dma((1,)),
                dma((4, tens)),
                dma((4, tens)),
                *[dma((4, most))] * 6,
            ],
            compiler_params=pltpu.CompilerParams(
                collective_id=0, has_side_effects=True, vmem_limit_bytes=36 * mib
            ),
            cost_estimate=pl.CostEstimate(
                flops=2 * rows * width * kw, bytes_accessed=2 * rows * width + 4 * width * kw, transcendentals=0
            ),
        )(*(
            pltpu.with_memory_space_constraint(x, pltpu.HBM)
            for x in (activations, cotangents, error_old, pause_positions, initial_q.T)
        ))
        error_new, q = pl.pallas_call(
            functools.partial(update_kernel, tile),
            out_shape=(
                jax.ShapeDtypeStruct(error_old.shape, BF16),
                jax.ShapeDtypeStruct((rank, kt), F32),
            ),
            in_specs=[vmem] * 4,
            out_specs=(hbm, vmem),
            scratch_shapes=[pltpu.VMEM((width, kw), BF16), dma((width // tile,))],
            compiler_params=pltpu.CompilerParams(vmem_limit_bytes=16 * mib),
        )(merged, pcat, qcat, own_q)
        return error_new, q.T

    return jax.shard_map(
        body,
        mesh=mesh,
        in_specs=(P("dp", "tensor"), P("dp", "tensor"), P(("dp", "tensor"), None), P(), P()),
        out_specs=(P(("dp", "tensor"), None), P("tensor", None)),
        check_vma=False,
    )
```

```python
import functools
import math

import jax
import jax.numpy as jnp
from jax import lax
from jax.experimental import pallas as pl
from jax.experimental.pallas import tpu as pltpu
from jax.sharding import PartitionSpec as P

F32 = jnp.float32
BF16 = jnp.bfloat16
NN = (((1,), (0,)), ((), ()))
NT = (((1,), (1,)), ((), ()))


def mm(a, b, dims):
    return lax.dot_general(a, b, dims, preferred_element_type=F32)


def mm_high(a, b, dims):
    return lax.dot_general(
        a, b, dims, preferred_element_type=F32, precision=lax.Precision.HIGHEST
    )


def pieces(x):
    high = x.astype(BF16)
    rest = x - high.astype(F32)
    middle = rest.astype(BF16)
    low = (rest - middle.astype(F32)).astype(BF16)
    return high, middle, low


def stacked(x):
    return jnp.concatenate(pieces(x), axis=0)


def folded(x):
    n = x.shape[0] // 3
    return x[:n] + x[n : 2 * n] + x[2 * n :]


def gram_of(x3):
    g = folded(mm(x3, x3, NT))
    n = g.shape[0]
    return g[:, :n] + g[:, n : 2 * n] + g[:, 2 * n :]


def applied(matrix, x3):
    return folded(mm(stacked(jnp.concatenate([matrix] * 3, axis=1)), x3, NN))


def inverse_cholesky(gram):
    n = gram.shape[0]
    rows = lax.broadcasted_iota(jnp.int32, (n, n), 0)
    cols = lax.broadcasted_iota(jnp.int32, (n, n), 1)
    left = gram
    right = jnp.where(rows == cols, 1.0, 0.0).astype(F32)
    pivots = jnp.ones((n, n), F32)
    group = math.gcd(n, 8)
    for k in range(n):
        if k % group == 0:
            spread = [jnp.broadcast_to(left[:, c : c + 1], (n, n)) for c in range(k, k + group)]
        column = spread[k % group]
        pivots = jnp.where(rows == k, column, pivots)
        scale = 1.0 / column[k : k + 1, :]
        column = jnp.where(rows > k, column, 0.0)
        for c in range(k % group + 1, group):
            entry = column[k - k % group + c : k - k % group + c + 1, :] * scale
            spread[c] = spread[c] - column * entry
        left_row = left[k : k + 1, :] * scale
        right_row = right[k : k + 1, :] * scale
        left = left - column * left_row
        right = right - column * right_row
    return right / jnp.sqrt(pivots)


def kernel(
    sizes, act_hbm, cot_hbm, err_hbm, pause_ref, q0_ref, merged, pcat, qcat, q_ref,
    act, cot, err, left_all, left3, parts, sum_in, qall,
    xa1, ra1, xb1, rb1, gd1, xa2, ra2, xb2, rb2, gd2, xa3, ra3, xb3, rb3, gd3,
    err_sem, act_sem, cot_sem, t_send, t_recv, s1, r1, s2, r2, s3, r3,
):
    replicas, outer, inner, tens, split, direct = sizes
    d = lax.axis_index("dp")
    t = lax.axis_index("tensor")
    o, i = d // inner, lax.rem(d, inner)
    row_count, width = act.shape
    kt = cot.shape[2]
    rank = q0_ref.shape[0]

    loads = err_sem.shape[0]
    load_cot = pltpu.make_async_copy(cot_hbm, cot.at[t], cot_sem.at[0])
    load_cot.start()

    def load(src, dst, sems):
        step = src.shape[0] // loads
        copies = []
        for n in range(loads):
            here = pl.ds(n * step, step)
            copies.append(pltpu.make_async_copy(src.at[here], dst.at[here], sems.at[n]))
        return copies

    load_err = load(err_hbm, err, err_sem)
    load_act = load(act_hbm, act, act_sem)
    for copy in load_err:
        copy.start()

    def outer_peer(k):
        return (lax.rem(o + k, outer) * inner + i, t)

    def inner_peer(k):
        return (o * inner + lax.rem(i + k, inner), t)

    def any_peer(k):
        return (lax.rem(d + k, replicas), t)

    def tensor_peer(k):
        return (d, lax.rem(t + k, tens))

    barrier = pltpu.get_barrier_semaphore()
    if direct:
        peers = [any_peer(k) for k in range(1, replicas)]
    else:
        peers = [outer_peer(k) for k in range(1, outer)]
        peers += [inner_peer(k) for k in range(1, inner)]
    peers += [tensor_peer(k) for k in range(1, tens)]
    for peer in peers:
        pl.semaphore_signal(barrier, inc=1, device_id=peer, device_id_type=pl.DeviceIdType.MESH)
    pl.semaphore_wait(barrier, len(peers))

    sent = []

    def send(src, dst, send_sem, recv_sem, peer):
        copy = pltpu.make_async_remote_copy(
            src_ref=src, dst_ref=dst, send_sem=send_sem, recv_sem=recv_sem,
            device_id=peer, device_id_type=pl.DeviceIdType.MESH,
        )
        copy.start()
        sent.append(copy)
        return copy

    cot_copies = [
        send(cot_hbm, cot.at[t], t_send.at[0, k], t_recv.at[0, k], tensor_peer(k))
        for k in range(1, tens)
    ]

    positions = lax.broadcasted_iota(jnp.int32, (row_count, pause_ref.shape[0]), 0)
    hits = jnp.sum(jnp.where(positions == pause_ref[...].reshape(1, -1), 1.0, 0.0), axis=1, keepdims=True)
    kept = jnp.where(hits == 0.0, 1.0, 0.0).astype(BF16)
    q3 = stacked(q0_ref[...])

    from_err = []
    step = width // loads
    for n, copy in enumerate(load_err):
        copy.wait()
        load_act[n].start()
        from_err.append(mm(q3, err[n * step : (n + 1) * step], NT))
    from_err = jnp.concatenate(from_err, axis=1)
    load_cot.wait()
    for copy in cot_copies:
        copy.wait_recv()
    for s in range(tens):
        cot[s] = cot[s] * kept
    tok = mm(q3[:, :kt], cot[0], NT)
    for s in range(1, tens):
        tok = tok + mm(q3[:, s * kt : (s + 1) * kt], cot[s], NT)
    tok3 = stacked(folded(tok))
    for copy in load_act:
        copy.wait()

    def left_part(first, last):
        whole = mm(tok3, act[:, first:last], NN) + from_err[:, first:last]
        return folded(whole) * (1.0 / replicas)

    tile = math.gcd(width, 256)

    def gradient_tiles(first, last):
        @pl.loop(first, last)
        def _(j):
            here = pl.ds(pl.multiple_of(j * tile, tile), tile)
            block = act[:, here].T
            for s in range(tens):
                outs = slice(s * kt, (s + 1) * kt)
                merged[here, outs] = mm(block, cot[s], NN) + err[here, outs].astype(F32)

    def all_reduce(value, bufs, ss, rs, first, second):
        (own1, n1, peer1), (own2, n2, peer2) = first, second
        xa, ra, xb, rb, gd = bufs
        h, span = xa.shape[1], value.shape[1]
        cw = xb.shape[2]
        if span < xa.shape[2]:
            xa[...] = jnp.zeros(xa.shape, F32)
        for p in range(n1):
            xa[p, :, :span] = value[p * h : (p + 1) * h]
        copies = [
            send(xa.at[lax.rem(own1 + k, n1)], ra.at[k], ss.at[0, k], rs.at[0, k], peer1(k))
            for k in range(1, n1)
        ]
        yield
        total = xa[own1]
        for k, copy in enumerate(copies, 1):
            copy.wait_recv()
            total = total + ra[k]
        if n2 > 1:
            for p in range(n2):
                xb[p] = total[:, p * cw : (p + 1) * cw]
            copies = [
                send(xb.at[lax.rem(own2 + k, n2)], rb.at[k], ss.at[1, k], rs.at[1, k], peer2(k))
                for k in range(1, n2)
            ]
            yield
            total = xb[own2]
            for k, copy in enumerate(copies, 1):
                copy.wait_recv()
                total = total + rb[k]
            gd[own1, own2] = total
            copies = [
                send(gd.at[own1, own2], gd.at[own1, own2], ss.at[2, k], rs.at[2, k], peer2(k))
                for k in range(1, n2)
            ]
            yield
            for copy in copies:
                copy.wait_recv()
        else:
            gd[own1, 0] = total
        copies = [
            send(gd.at[own1], gd.at[own1], ss.at[3, k], rs.at[3, k], peer1(k))
            for k in range(1, n1)
        ]
        yield
        for copy in copies:
            copy.wait_recv()
        bands = [
            jnp.concatenate([gd[p, c] for c in range(n2)], axis=1)[:, :span]
            for p in range(n1)
        ]
        yield jnp.concatenate(bands, axis=0)

    by_inner = (i, inner, inner_peer)
    by_outer = (o, outer, outer_peer)
    tiles = width // tile
    marks = [tiles * n // 10 for n in (0, 3, 5, 7, 9)]
    run1 = all_reduce(left_part(0, split), (xa1, ra1, xb1, rb1, gd1), s1, r1, by_outer, by_inner)
    next(run1)
    run2 = all_reduce(left_part(split, width), (xa2, ra2, xb2, rb2, gd2), s2, r2, by_inner, by_outer)
    next(run2)
    for n in range(4):
        gradient_tiles(marks[n], marks[n + 1])
        part2 = next(run2)
        part1 = next(run1)
    left = jnp.concatenate([part1, part2], axis=1)
    left_all[t] = left
    left_copies = [
        send(left_all.at[t], left_all.at[t], t_send.at[1, k], t_recv.at[1, k], tensor_peer(k))
        for k in range(1, tens)
    ]

    own3 = stacked(left)
    left3[t] = own3
    v3 = stacked(folded(mm(own3, act[...], NT)))
    for copy in left_copies:
        copy.wait_recv()
    for k in range(1, tens):
        peer = lax.rem(t + k, tens)
        left3[peer] = stacked(left_all[peer])
    gram = gram_of(left3[0])
    for s in range(1, tens):
        gram = gram + gram_of(left3[s])
    inv1 = inverse_cholesky(gram)
    s_err = mm(left3[t], err[...], NN)
    for s in range(tens):
        total = s_err[:, s * kt : (s + 1) * kt] + mm(v3, cot[s], NN)
        parts[s] = folded(total) * (1.0 / replicas)
    copies = [
        send(parts.at[lax.rem(t + k, tens)], sum_in.at[k], t_send.at[2, k], t_recv.at[2, k], tensor_peer(k))
        for k in range(1, tens)
    ]
    held = {}

    def second_gram():
        gram = jnp.zeros((rank, rank), F32)
        for s in range(tens):
            basis3 = stacked(applied(inv1, left3[s]))
            left3[s] = basis3
            gram = gram + gram_of(basis3)
        held["gram"] = gram

    def second_inverse():
        held["inv2"] = inverse_cholesky(held["gram"])
        held["both"] = mm_high(held["inv2"], inv1, NN)

    def own_basis():
        high, middle, _ = pieces(applied(held["inv2"], left3[t]))
        pcat[...] = jnp.concatenate([high, middle, high], axis=0)

    second_gram()
    total = parts[t]
    for k, copy in enumerate(copies, 1):
        copy.wait_recv()
        total = total + sum_in[k]
    groups = ((d, replicas, any_peer), (0, 1, None)) if direct else (by_inner, by_outer)
    run3 = all_reduce(total, (xa3, ra3, xb3, rb3, gd3), s3, r3, *groups)
    next(run3)
    second_inverse()
    total = next(run3)
    own_basis()
    while total is None:
        total = next(run3)
    own_q = mm_high(held["both"], total, NN)
    qall[t] = own_q
    copies = [
        send(qall.at[t], qall.at[t], t_send.at[3, k], t_recv.at[3, k], tensor_peer(k))
        for k in range(1, tens)
    ]
    q_ref[...] = own_q
    gradient_tiles(marks[4], tiles)
    for copy in copies:
        copy.wait_recv()
    for s in range(tens):
        high, middle, _ = pieces(qall[s])
        qcat[s] = jnp.concatenate([high, high, middle], axis=0)
    for copy in sent:
        copy.wait_send()


def update_kernel(tile, merged, pcat, qcat, q_in, out_hbm, q_out, out, sems):
    tens, _, kt = qcat.shape
    copies = []
    for j in range(out.shape[0] // tile):
        here = slice(j * tile, (j + 1) * tile)
        basis = pcat[:, here].T
        for s in range(tens):
            outs = slice(s * kt, (s + 1) * kt)
            update = mm(basis, qcat[s], NN)
            out[here, outs] = (merged[here, outs] - update).astype(BF16)
        copy = pltpu.make_async_copy(out.at[here], out_hbm.at[here], sems.at[j])
        copy.start()
        copies.append(copy)
    q_out[...] = q_in[...]
    for copy in copies:
        copy.wait()


def solution(mesh):
    replicas, tens = mesh.shape["dp"], mesh.shape["tensor"]
    inner = 1
    while inner * inner < replicas or replicas % inner:
        inner += 1
    outer = replicas // inner

    def body(activations, cotangents, error_old, pause_positions, initial_q):
        rows, width = activations.shape
        kt = cotangents.shape[1]
        kw, rank = initial_q.shape
        mib = 1024 * 1024
        tile = math.gcd(width, 256)
        split = 2 * width // 5 // 128 * 128
        direct = replicas <= min(rank, 16)
        loads = 4 if width % 512 == 0 and rows % 64 == 0 else 1

        def reduce_bufs(span, n1, n2):
            h, cw = rank // n1, -(-span // (128 * n2)) * 128
            return [
                pltpu.VMEM((n1, h, cw * n2), F32),
                pltpu.VMEM((n1, h, cw * n2), F32),
                pltpu.VMEM((n2, h, cw), F32),
                pltpu.VMEM((n2, h, cw), F32),
                pltpu.VMEM((n1, n2, h, cw), F32),
            ]

        most = replicas if direct else max(inner, outer)
        hbm = pl.BlockSpec(memory_space=pltpu.HBM)
        vmem = pl.BlockSpec(memory_space=pltpu.VMEM)
        dma = pltpu.SemaphoreType.DMA
        merged, pcat, qcat, own_q = pl.pallas_call(
            functools.partial(kernel, (replicas, outer, inner, tens, split, direct)),
            out_shape=(
                pltpu.VMEM((width, kw), F32),
                pltpu.VMEM((3 * rank, width), BF16),
                pltpu.VMEM((tens, 3 * rank, kt), BF16),
                pltpu.VMEM((rank, kt), F32),
            ),
            in_specs=[hbm, hbm, hbm, vmem, vmem],
            out_specs=(vmem,) * 4,
            scratch_shapes=[
                pltpu.VMEM((rows, width), BF16),
                pltpu.VMEM((tens, rows, kt), BF16),
                pltpu.VMEM((width, kw), BF16),
                pltpu.VMEM((tens, rank, width), F32),
                pltpu.VMEM((tens, 3 * rank, width), BF16),
                pltpu.VMEM((tens, rank, kt), F32),
                pltpu.VMEM((tens, rank, kt), F32),
                pltpu.VMEM((tens, rank, kt), F32),
                *reduce_bufs(split, outer, inner),
                *reduce_bufs(width - split, inner, outer),
                *(reduce_bufs(kt, replicas, 1) if direct else reduce_bufs(kt, inner, outer)),
                dma((loads,)),
                dma((loads,)),
                dma((1,)),
                dma((4, tens)),
                dma((4, tens)),
                *[dma((4, most))] * 6,
            ],
            compiler_params=pltpu.CompilerParams(
                collective_id=0, has_side_effects=True, vmem_limit_bytes=36 * mib
            ),
            cost_estimate=pl.CostEstimate(
                flops=2 * rows * width * kw, bytes_accessed=2 * rows * width + 4 * width * kw, transcendentals=0
            ),
        )(*(
            pltpu.with_memory_space_constraint(x, pltpu.HBM)
            for x in (activations, cotangents, error_old, pause_positions, initial_q.T)
        ))
        error_new, q = pl.pallas_call(
            functools.partial(update_kernel, tile),
            out_shape=(
                jax.ShapeDtypeStruct(error_old.shape, BF16),
                jax.ShapeDtypeStruct((rank, kt), F32),
            ),
            in_specs=[vmem] * 4,
            out_specs=(hbm, vmem),
            scratch_shapes=[pltpu.VMEM((width, kw), BF16), dma((width // tile,))],
            compiler_params=pltpu.CompilerParams(vmem_limit_bytes=16 * mib),
        )(merged, pcat, qcat, own_q)
        return error_new, q.T

    return jax.shard_map(
        body,
        mesh=mesh,
        in_specs=(P("dp", "tensor"), P("dp", "tensor"), P(("dp", "tensor"), None), P(), P()),
        out_specs=(P(("dp", "tensor"), None), P("tensor", None)),
        check_vma=False,
    )
```

```python
import functools
import math

import jax
import jax.numpy as jnp
from jax import lax
from jax.experimental import pallas as pl
from jax.experimental.pallas import tpu as pltpu
from jax.sharding import PartitionSpec as P

F32 = jnp.float32
BF16 = jnp.bfloat16
NN = (((1,), (0,)), ((), ()))
NT = (((1,), (1,)), ((), ()))


def mm(a, b, dims):
    return lax.dot_general(a, b, dims, preferred_element_type=F32)


def mm_high(a, b, dims):
    return lax.dot_general(
        a, b, dims, preferred_element_type=F32, precision=lax.Precision.HIGHEST
    )


def pieces(x):
    high = x.astype(BF16)
    rest = x - high.astype(F32)
    middle = rest.astype(BF16)
    low = (rest - middle.astype(F32)).astype(BF16)
    return high, middle, low


def stacked(x):
    return jnp.concatenate(pieces(x), axis=0)


def folded(x):
    n = x.shape[0] // 3
    return x[:n] + x[n : 2 * n] + x[2 * n :]


def gram_of(x3):
    g = folded(mm(x3, x3, NT))
    n = g.shape[0]
    return g[:, :n] + g[:, n : 2 * n] + g[:, 2 * n :]


def applied(matrix, x3):
    return folded(mm(stacked(jnp.concatenate([matrix] * 3, axis=1)), x3, NN))


def inverse_cholesky(gram):
    n = gram.shape[0]
    rows = lax.broadcasted_iota(jnp.int32, (n, n), 0)
    cols = lax.broadcasted_iota(jnp.int32, (n, n), 1)
    left = gram
    right = jnp.where(rows == cols, 1.0, 0.0).astype(F32)
    pivots = jnp.ones((n, n), F32)
    group = math.gcd(n, 8)
    for k in range(n):
        if k % group == 0:
            spread = [jnp.broadcast_to(left[:, c : c + 1], (n, n)) for c in range(k, k + group)]
        column = spread[k % group]
        pivots = jnp.where(rows == k, column, pivots)
        scale = 1.0 / column[k : k + 1, :]
        column = jnp.where(rows > k, column, 0.0)
        for c in range(k % group + 1, group):
            entry = column[k - k % group + c : k - k % group + c + 1, :] * scale
            spread[c] = spread[c] - column * entry
        left_row = left[k : k + 1, :] * scale
        right_row = right[k : k + 1, :] * scale
        left = left - column * left_row
        right = right - column * right_row
    return right / jnp.sqrt(pivots)


def kernel(
    sizes, act_hbm, cot_hbm, err_hbm, pause_ref, q0_ref, merged, pcat, qcat, q_ref,
    act, cot, err, q3, left_all, left3, parts, sum_in, qall,
    xa1, ra1, xb1, rb1, gd1, xa2, ra2, xb2, rb2, gd2, xa3, ra3, xb3, rb3, gd3,
    err_sem, act_sem, cot_sem, t_send, t_recv, s1, r1, s2, r2, s3, r3,
):
    replicas, outer, inner, tens, split, direct = sizes
    d = lax.axis_index("dp")
    t = lax.axis_index("tensor")
    o, i = d // inner, lax.rem(d, inner)
    row_count, width = act.shape
    kt = cot.shape[2]
    rank = q0_ref.shape[0]

    loads = err_sem.shape[0]
    load_cot = pltpu.make_async_copy(cot_hbm, cot.at[t], cot_sem.at[0])
    load_cot.start()

    def load(src, dst, sems):
        step = src.shape[0] // loads
        copies = []
        for n in range(loads):
            here = pl.ds(n * step, step)
            copies.append(pltpu.make_async_copy(src.at[here], dst.at[here], sems.at[n]))
        return copies

    load_err = load(err_hbm, err, err_sem)
    load_act = load(act_hbm, act, act_sem)
    for copy in load_err:
        copy.start()

    def outer_peer(k):
        return (lax.rem(o + k, outer) * inner + i, t)

    def inner_peer(k):
        return (o * inner + lax.rem(i + k, inner), t)

    def any_peer(k):
        return (lax.rem(d + k, replicas), t)

    def tensor_peer(k):
        return (d, lax.rem(t + k, tens))

    barrier = pltpu.get_barrier_semaphore()
    if direct:
        peers = [any_peer(k) for k in range(1, replicas)]
    else:
        peers = [outer_peer(k) for k in range(1, outer)]
        peers += [inner_peer(k) for k in range(1, inner)]
    peers += [tensor_peer(k) for k in range(1, tens)]
    for peer in peers:
        pl.semaphore_signal(barrier, inc=1, device_id=peer, device_id_type=pl.DeviceIdType.MESH)
    pl.semaphore_wait(barrier, len(peers))

    sent = []

    def send(src, dst, send_sem, recv_sem, peer):
        copy = pltpu.make_async_remote_copy(
            src_ref=src, dst_ref=dst, send_sem=send_sem, recv_sem=recv_sem,
            device_id=peer, device_id_type=pl.DeviceIdType.MESH,
        )
        copy.start()
        sent.append(copy)
        return copy

    cot_copies = [
        send(cot_hbm, cot.at[t], t_send.at[0, k], t_recv.at[0, k], tensor_peer(k))
        for k in range(1, tens)
    ]

    positions = lax.broadcasted_iota(jnp.int32, (row_count, pause_ref.shape[0]), 0)
    hits = jnp.sum(jnp.where(positions == pause_ref[...].reshape(1, -1), 1.0, 0.0), axis=1, keepdims=True)
    kept = jnp.where(hits == 0.0, 1.0, 0.0).astype(BF16)
    q3[...] = stacked(q0_ref[...])

    from_err = []
    step = width // loads
    for n, copy in enumerate(load_err):
        copy.wait()
        load_act[n].start()
        from_err.append(mm(q3[...], err[n * step : (n + 1) * step], NT))
    from_err = jnp.concatenate(from_err, axis=1)
    load_cot.wait()

    def token_sums(s):
        cot[s] = cot[s] * kept
        outs = pl.ds(pl.multiple_of(s * kt, kt), kt)
        return mm(q3[:, outs], cot[s], NT)

    tok = token_sums(t)
    for k, copy in enumerate(cot_copies, 1):
        copy.wait_recv()
        tok = tok + token_sums(lax.rem(t + tens - k, tens))
    tok3 = stacked(folded(tok))
    for copy in load_act:
        copy.wait()

    def left_part(first, last):
        whole = mm(tok3, act[:, first:last], NN) + from_err[:, first:last]
        return folded(whole) * (1.0 / replicas)

    tile = width // 5 if width % 640 == 0 else math.gcd(width, 256)
    tiles = width // tile

    def gradient_tiles(first, last):
        for j in range(first, last):
            here = slice(j * tile, (j + 1) * tile)
            block = act[:, here].T
            for s in range(tens):
                outs = slice(s * kt, (s + 1) * kt)
                merged[here, outs] = mm(block, cot[s], NN) + err[here, outs].astype(F32)

    def all_reduce(value, bufs, ss, rs, first, second):
        (own1, n1, peer1), (own2, n2, peer2) = first, second
        xa, ra, xb, rb, gd = bufs
        h, span = xa.shape[1], value.shape[1]
        cw = xb.shape[2]
        if span < xa.shape[2]:
            xa[...] = jnp.zeros(xa.shape, F32)
        for p in range(n1):
            xa[p, :, :span] = value[p * h : (p + 1) * h]
        copies = [
            send(xa.at[lax.rem(own1 + k, n1)], ra.at[k], ss.at[0, k], rs.at[0, k], peer1(k))
            for k in range(1, n1)
        ]
        yield
        total = xa[own1]
        for k, copy in enumerate(copies, 1):
            copy.wait_recv()
            total = total + ra[k]
        if n2 > 1:
            for p in range(n2):
                xb[p] = total[:, p * cw : (p + 1) * cw]
            copies = [
                send(xb.at[lax.rem(own2 + k, n2)], rb.at[k], ss.at[1, k], rs.at[1, k], peer2(k))
                for k in range(1, n2)
            ]
            yield
            total = xb[own2]
            for k, copy in enumerate(copies, 1):
                copy.wait_recv()
                total = total + rb[k]
            gd[own1, own2] = total
            copies = [
                send(gd.at[own1, own2], gd.at[own1, own2], ss.at[2, k], rs.at[2, k], peer2(k))
                for k in range(1, n2)
            ]
            yield
            for copy in copies:
                copy.wait_recv()
        else:
            gd[own1, 0] = total
        copies = [
            send(gd.at[own1], gd.at[own1], ss.at[3, k], rs.at[3, k], peer1(k))
            for k in range(1, n1)
        ]
        yield
        for copy in copies:
            copy.wait_recv()
        bands = [
            jnp.concatenate([gd[p, c] for c in range(n2)], axis=1)[:, :span]
            for p in range(n1)
        ]
        yield jnp.concatenate(bands, axis=0)

    by_inner = (i, inner, inner_peer)
    by_outer = (o, outer, outer_peer)
    marks = [tiles * n // 5 for n in range(5)]
    run1 = all_reduce(left_part(0, split), (xa1, ra1, xb1, rb1, gd1), s1, r1, by_outer, by_inner)
    next(run1)
    run2 = all_reduce(left_part(split, width), (xa2, ra2, xb2, rb2, gd2), s2, r2, by_inner, by_outer)
    next(run2)
    for n in range(4):
        gradient_tiles(marks[n], marks[n + 1])
        part2 = next(run2)
        part1 = next(run1)
    left = jnp.concatenate([part1, part2], axis=1)
    left_all[t] = left
    left_copies = [
        send(left_all.at[t], left_all.at[t], t_send.at[1, k], t_recv.at[1, k], tensor_peer(k))
        for k in range(1, tens)
    ]

    own3 = stacked(left)
    left3[t] = own3
    v3 = stacked(folded(mm(own3, act[...], NT)))
    for copy in left_copies:
        copy.wait_recv()
    for k in range(1, tens):
        peer = lax.rem(t + k, tens)
        left3[peer] = stacked(left_all[peer])
    gram = gram_of(left3[0])
    for s in range(1, tens):
        gram = gram + gram_of(left3[s])
    inv1 = inverse_cholesky(gram)
    s_err = mm(left3[t], err[...], NN)
    for s in range(tens):
        total = s_err[:, s * kt : (s + 1) * kt] + mm(v3, cot[s], NN)
        parts[s] = folded(total) * (1.0 / replicas)
    copies = [
        send(parts.at[lax.rem(t + k, tens)], sum_in.at[k], t_send.at[2, k], t_recv.at[2, k], tensor_peer(k))
        for k in range(1, tens)
    ]
    held = {}

    def second_gram():
        gram = jnp.zeros((rank, rank), F32)
        for s in range(tens):
            basis3 = stacked(applied(inv1, left3[s]))
            left3[s] = basis3
            gram = gram + gram_of(basis3)
        held["gram"] = gram

    def second_inverse():
        held["inv2"] = inverse_cholesky(held["gram"])
        held["both"] = mm_high(held["inv2"], inv1, NN)

    def own_basis():
        high, middle, _ = pieces(applied(held["inv2"], left3[t]))
        pcat[...] = jnp.concatenate([high, middle, high], axis=0)

    second_gram()
    total = parts[t]
    for k, copy in enumerate(copies, 1):
        copy.wait_recv()
        total = total + sum_in[k]
    groups = ((d, replicas, any_peer), (0, 1, None)) if direct else (by_inner, by_outer)
    run3 = all_reduce(total, (xa3, ra3, xb3, rb3, gd3), s3, r3, *groups)
    next(run3)
    second_inverse()
    total = next(run3)
    own_basis()
    while total is None:
        total = next(run3)
    own_q = mm_high(held["both"], total, NN)
    qall[t] = own_q
    copies = [
        send(qall.at[t], qall.at[t], t_send.at[3, k], t_recv.at[3, k], tensor_peer(k))
        for k in range(1, tens)
    ]
    q_ref[...] = own_q
    gradient_tiles(marks[4], tiles)
    for copy in copies:
        copy.wait_recv()
    for s in range(tens):
        high, middle, _ = pieces(qall[s])
        qcat[s] = jnp.concatenate([high, high, middle], axis=0)
    for copy in sent:
        copy.wait_send()


def update_kernel(tile, merged, pcat, qcat, q_in, out_hbm, q_out, out, sems):
    tens, _, kt = qcat.shape
    copies = []
    for j in range(out.shape[0] // tile):
        here = slice(j * tile, (j + 1) * tile)
        basis = pcat[:, here].T
        for s in range(tens):
            outs = slice(s * kt, (s + 1) * kt)
            update = mm(basis, qcat[s], NN)
            out[here, outs] = (merged[here, outs] - update).astype(BF16)
        copy = pltpu.make_async_copy(out.at[here], out_hbm.at[here], sems.at[j])
        copy.start()
        copies.append(copy)
    q_out[...] = q_in[...]
    for copy in copies:
        copy.wait()


def solution(mesh):
    replicas, tens = mesh.shape["dp"], mesh.shape["tensor"]
    inner = 1
    while inner * inner < replicas or replicas % inner:
        inner += 1
    outer = replicas // inner

    def body(activations, cotangents, error_old, pause_positions, initial_q):
        rows, width = activations.shape
        kt = cotangents.shape[1]
        kw, rank = initial_q.shape
        mib = 1024 * 1024
        tile = math.gcd(width, 256)
        split = 2 * width // 5 // 128 * 128
        direct = replicas <= min(rank, 16)
        loads = 4 if width % 512 == 0 and rows % 64 == 0 else 1

        def reduce_bufs(span, n1, n2):
            h, cw = rank // n1, -(-span // (128 * n2)) * 128
            return [
                pltpu.VMEM((n1, h, cw * n2), F32),
                pltpu.VMEM((n1, h, cw * n2), F32),
                pltpu.VMEM((n2, h, cw), F32),
                pltpu.VMEM((n2, h, cw), F32),
                pltpu.VMEM((n1, n2, h, cw), F32),
            ]

        most = replicas if direct else max(inner, outer)
        hbm = pl.BlockSpec(memory_space=pltpu.HBM)
        vmem = pl.BlockSpec(memory_space=pltpu.VMEM)
        dma = pltpu.SemaphoreType.DMA
        merged, pcat, qcat, own_q = pl.pallas_call(
            functools.partial(kernel, (replicas, outer, inner, tens, split, direct)),
            out_shape=(
                pltpu.VMEM((width, kw), F32),
                pltpu.VMEM((3 * rank, width), BF16),
                pltpu.VMEM((tens, 3 * rank, kt), BF16),
                pltpu.VMEM((rank, kt), F32),
            ),
            in_specs=[hbm, hbm, hbm, vmem, vmem],
            out_specs=(vmem,) * 4,
            scratch_shapes=[
                pltpu.VMEM((rows, width), BF16),
                pltpu.VMEM((tens, rows, kt), BF16),
                pltpu.VMEM((width, kw), BF16),
                pltpu.VMEM((3 * rank, kw), BF16),
                pltpu.VMEM((tens, rank, width), F32),
                pltpu.VMEM((tens, 3 * rank, width), BF16),
                pltpu.VMEM((tens, rank, kt), F32),
                pltpu.VMEM((tens, rank, kt), F32),
                pltpu.VMEM((tens, rank, kt), F32),
                *reduce_bufs(split, outer, inner),
                *reduce_bufs(width - split, inner, outer),
                *(reduce_bufs(kt, replicas, 1) if direct else reduce_bufs(kt, inner, outer)),
                dma((loads,)),
                dma((loads,)),
                dma((1,)),
                dma((4, tens)),
                dma((4, tens)),
                *[dma((4, most))] * 6,
            ],
            compiler_params=pltpu.CompilerParams(
                collective_id=0, has_side_effects=True, vmem_limit_bytes=36 * mib
            ),
            cost_estimate=pl.CostEstimate(
                flops=2 * rows * width * kw, bytes_accessed=2 * rows * width + 4 * width * kw, transcendentals=0
            ),
        )(*(
            pltpu.with_memory_space_constraint(x, pltpu.HBM)
            for x in (activations, cotangents, error_old, pause_positions, initial_q.T)
        ))
        error_new, q = pl.pallas_call(
            functools.partial(update_kernel, tile),
            out_shape=(
                jax.ShapeDtypeStruct(error_old.shape, BF16),
                jax.ShapeDtypeStruct((rank, kt), F32),
            ),
            in_specs=[vmem] * 4,
            out_specs=(hbm, vmem),
            scratch_shapes=[pltpu.VMEM((width, kw), BF16), dma((width // tile,))],
            compiler_params=pltpu.CompilerParams(vmem_limit_bytes=16 * mib),
        )(merged, pcat, qcat, own_q)
        return error_new, q.T

    return jax.shard_map(
        body,
        mesh=mesh,
        in_specs=(P("dp", "tensor"), P("dp", "tensor"), P(("dp", "tensor"), None), P(), P()),
        out_specs=(P(("dp", "tensor"), None), P("tensor", None)),
        check_vma=False,
    )
```

```python
import functools
import math

import jax
import jax.numpy as jnp
from jax import lax
from jax.experimental import pallas as pl
from jax.experimental.pallas import tpu as pltpu
from jax.sharding import PartitionSpec as P

F32 = jnp.float32
BF16 = jnp.bfloat16
NN = (((1,), (0,)), ((), ()))
NT = (((1,), (1,)), ((), ()))


def mm(a, b, dims):
    return lax.dot_general(a, b, dims, preferred_element_type=F32)


def mm_high(a, b, dims):
    return lax.dot_general(
        a, b, dims, preferred_element_type=F32, precision=lax.Precision.HIGHEST
    )


def pieces(x):
    high = x.astype(BF16)
    rest = x - high.astype(F32)
    middle = rest.astype(BF16)
    low = (rest - middle.astype(F32)).astype(BF16)
    return high, middle, low


def stacked(x):
    return jnp.concatenate(pieces(x), axis=0)


def folded(x):
    n = x.shape[0] // 3
    return x[:n] + x[n : 2 * n] + x[2 * n :]


def gram_of(x3):
    g = folded(mm(x3, x3, NT))
    n = g.shape[0]
    return g[:, :n] + g[:, n : 2 * n] + g[:, 2 * n :]


def applied(matrix, x3):
    return folded(mm(stacked(jnp.concatenate([matrix] * 3, axis=1)), x3, NN))


def inverse_cholesky(gram):
    n = gram.shape[0]
    rows = lax.broadcasted_iota(jnp.int32, (n, n), 0)
    cols = lax.broadcasted_iota(jnp.int32, (n, n), 1)
    left = gram
    right = jnp.where(rows == cols, 1.0, 0.0).astype(F32)
    pivots = jnp.ones((n, n), F32)
    group = math.gcd(n, 8)
    for k in range(n):
        if k % group == 0:
            spread = [jnp.broadcast_to(left[:, c : c + 1], (n, n)) for c in range(k, k + group)]
        column = spread[k % group]
        pivots = jnp.where(rows == k, column, pivots)
        scale = 1.0 / column[k : k + 1, :]
        column = jnp.where(rows > k, column, 0.0)
        for c in range(k % group + 1, group):
            entry = column[k - k % group + c : k - k % group + c + 1, :] * scale
            spread[c] = spread[c] - column * entry
        left_row = left[k : k + 1, :] * scale
        right_row = right[k : k + 1, :] * scale
        left = left - column * left_row
        right = right - column * right_row
    return right / jnp.sqrt(pivots)


def kernel(
    sizes, act_hbm, cot_hbm, err_hbm, pause_ref, q0_ref, merged, pcat, qcat, q_ref,
    act, cot, err, q3, turned, left_all, left3, parts, sum_in, qall,
    xa1, ra1, xb1, rb1, gd1, xa2, ra2, xb2, rb2, gd2, xa3, ra3, xb3, rb3, gd3,
    err_sem, act_sem, cot_sem, t_send, t_recv, s1, r1, s2, r2, s3, r3,
):
    replicas, outer, inner, tens, split, direct = sizes
    d = lax.axis_index("dp")
    t = lax.axis_index("tensor")
    o, i = d // inner, lax.rem(d, inner)
    row_count, width = act.shape
    kt = cot.shape[2]
    rank = q0_ref.shape[0]

    loads = err_sem.shape[0]
    load_cot = pltpu.make_async_copy(cot_hbm, cot.at[t], cot_sem.at[0])
    load_cot.start()

    def load(src, dst, sems):
        step = src.shape[0] // loads
        copies = []
        for n in range(loads):
            here = pl.ds(n * step, step)
            copies.append(pltpu.make_async_copy(src.at[here], dst.at[here], sems.at[n]))
        return copies

    load_err = load(err_hbm, err, err_sem)
    load_act = load(act_hbm, act, act_sem)
    for copy in load_err:
        copy.start()

    def outer_peer(k):
        return (lax.rem(o + k, outer) * inner + i, t)

    def inner_peer(k):
        return (o * inner + lax.rem(i + k, inner), t)

    def any_peer(k):
        return (lax.rem(d + k, replicas), t)

    def tensor_peer(k):
        return (d, lax.rem(t + k, tens))

    barrier = pltpu.get_barrier_semaphore()
    if direct:
        peers = [any_peer(k) for k in range(1, replicas)]
    else:
        peers = [outer_peer(k) for k in range(1, outer)]
        peers += [inner_peer(k) for k in range(1, inner)]
    peers += [tensor_peer(k) for k in range(1, tens)]
    for peer in peers:
        pl.semaphore_signal(barrier, inc=1, device_id=peer, device_id_type=pl.DeviceIdType.MESH)
    pl.semaphore_wait(barrier, len(peers))

    sent = []

    def send(src, dst, send_sem, recv_sem, peer):
        copy = pltpu.make_async_remote_copy(
            src_ref=src, dst_ref=dst, send_sem=send_sem, recv_sem=recv_sem,
            device_id=peer, device_id_type=pl.DeviceIdType.MESH,
        )
        copy.start()
        sent.append(copy)
        return copy

    cot_copies = [
        send(cot_hbm, cot.at[t], t_send.at[0, k], t_recv.at[0, k], tensor_peer(k))
        for k in range(1, tens)
    ]

    positions = lax.broadcasted_iota(jnp.int32, (row_count, pause_ref.shape[0]), 0)
    hits = jnp.sum(jnp.where(positions == pause_ref[...].reshape(1, -1), 1.0, 0.0), axis=1, keepdims=True)
    kept = jnp.where(hits == 0.0, 1.0, 0.0).astype(BF16)
    q3[...] = stacked(q0_ref[...])

    def token_sums(s):
        cot[s] = cot[s] * kept
        outs = pl.ds(pl.multiple_of(s * kt, kt), kt)
        return mm(q3[:, outs], cot[s], NT)

    load_cot.wait()
    tok = token_sums(t)
    from_err = []
    step = width // loads
    for n, copy in enumerate(load_err):
        copy.wait()
        load_act[n].start()
        from_err.append(mm(q3[...], err[n * step : (n + 1) * step], NT))
    from_err = jnp.concatenate(from_err, axis=1)
    for k, copy in enumerate(cot_copies, 1):
        copy.wait_recv()
        tok = tok + token_sums(lax.rem(t + tens - k, tens))
    tok3 = stacked(folded(tok))
    for copy in load_act:
        copy.wait()

    def left_part(first, last):
        whole = mm(tok3, act[:, first:last], NN) + from_err[:, first:last]
        return folded(whole) * (1.0 / replicas)

    tile = math.gcd(width, 256)
    tiles = width // tile

    def gradient_tiles(first, last):
        @pl.loop(first, last)
        def _(j):
            here = pl.ds(pl.multiple_of(j * tile, tile), tile)
            block = act[:, here].T
            turned[here] = block
            for s in range(tens):
                outs = slice(s * kt, (s + 1) * kt)
                merged[here, outs] = mm(block, cot[s], NN) + err[here, outs].astype(F32)

    def all_reduce(value, bufs, ss, rs, first, second):
        (own1, n1, peer1), (own2, n2, peer2) = first, second
        xa, ra, xb, rb, gd = bufs
        h, span = xa.shape[1], value.shape[1]
        cw = xb.shape[2]
        if span < xa.shape[2]:
            xa[...] = jnp.zeros(xa.shape, F32)
        for p in range(n1):
            xa[p, :, :span] = value[p * h : (p + 1) * h]
        copies = [
            send(xa.at[lax.rem(own1 + k, n1)], ra.at[k], ss.at[0, k], rs.at[0, k], peer1(k))
            for k in range(1, n1)
        ]
        yield
        total = xa[own1]
        for k, copy in enumerate(copies, 1):
            copy.wait_recv()
            total = total + ra[k]
        if n2 > 1:
            for p in range(n2):
                xb[p] = total[:, p * cw : (p + 1) * cw]
            copies = [
                send(xb.at[lax.rem(own2 + k, n2)], rb.at[k], ss.at[1, k], rs.at[1, k], peer2(k))
                for k in range(1, n2)
            ]
            yield
            total = xb[own2]
            for k, copy in enumerate(copies, 1):
                copy.wait_recv()
                total = total + rb[k]
            gd[own1, own2] = total
            copies = [
                send(gd.at[own1, own2], gd.at[own1, own2], ss.at[2, k], rs.at[2, k], peer2(k))
                for k in range(1, n2)
            ]
            yield
            for copy in copies:
                copy.wait_recv()
        else:
            gd[own1, 0] = total
        copies = [
            send(gd.at[own1], gd.at[own1], ss.at[3, k], rs.at[3, k], peer1(k))
            for k in range(1, n1)
        ]
        yield
        for copy in copies:
            copy.wait_recv()
        bands = [
            jnp.concatenate([gd[p, c] for c in range(n2)], axis=1)[:, :span]
            for p in range(n1)
        ]
        yield jnp.concatenate(bands, axis=0)

    by_inner = (i, inner, inner_peer)
    by_outer = (o, outer, outer_peer)
    marks = [tiles * n // 10 for n in (0, 3, 5, 7, 10)]
    run1 = all_reduce(left_part(0, split), (xa1, ra1, xb1, rb1, gd1), s1, r1, by_outer, by_inner)
    next(run1)
    run2 = all_reduce(left_part(split, width), (xa2, ra2, xb2, rb2, gd2), s2, r2, by_inner, by_outer)
    next(run2)
    for n in range(4):
        gradient_tiles(marks[n], marks[n + 1])
        part2 = next(run2)
        part1 = next(run1)
    left = jnp.concatenate([part1, part2], axis=1)
    left_all[t] = left
    left_copies = [
        send(left_all.at[t], left_all.at[t], t_send.at[1, k], t_recv.at[1, k], tensor_peer(k))
        for k in range(1, tens)
    ]

    own3 = stacked(left)
    left3[t] = own3
    v3 = stacked(folded(mm(own3, turned[...], NN)))
    for copy in left_copies:
        copy.wait_recv()
    for k in range(1, tens):
        peer = lax.rem(t + k, tens)
        left3[peer] = stacked(left_all[peer])
    gram = gram_of(left3[0])
    for s in range(1, tens):
        gram = gram + gram_of(left3[s])
    inv1 = inverse_cholesky(gram)
    s_err = mm(left3[t], err[...], NN)
    for s in range(tens):
        total = s_err[:, s * kt : (s + 1) * kt] + mm(v3, cot[s], NN)
        parts[s] = folded(total) * (1.0 / replicas)
    copies = [
        send(parts.at[lax.rem(t + k, tens)], sum_in.at[k], t_send.at[2, k], t_recv.at[2, k], tensor_peer(k))
        for k in range(1, tens)
    ]
    held = {}

    def second_gram():
        gram = jnp.zeros((rank, rank), F32)
        for s in range(tens):
            basis3 = stacked(applied(inv1, left3[s]))
            left3[s] = basis3
            gram = gram + gram_of(basis3)
        held["gram"] = gram

    def second_inverse():
        held["inv2"] = inverse_cholesky(held["gram"])
        held["both"] = mm_high(held["inv2"], inv1, NN)

    def own_basis():
        high, middle, _ = pieces(applied(held["inv2"], left3[t]))
        pcat[...] = jnp.concatenate([high, middle, high], axis=0)

    second_gram()
    total = parts[t]
    for k, copy in enumerate(copies, 1):
        copy.wait_recv()
        total = total + sum_in[k]
    groups = ((d, replicas, any_peer), (0, 1, None)) if direct else (by_inner, by_outer)
    run3 = all_reduce(total, (xa3, ra3, xb3, rb3, gd3), s3, r3, *groups)
    next(run3)
    second_inverse()
    total = next(run3)
    own_basis()
    while total is None:
        total = next(run3)
    own_q = mm_high(held["both"], total, NN)
    qall[t] = own_q
    copies = [
        send(qall.at[t], qall.at[t], t_send.at[3, k], t_recv.at[3, k], tensor_peer(k))
        for k in range(1, tens)
    ]
    q_ref[...] = own_q
    for copy in copies:
        copy.wait_recv()
    for s in range(tens):
        high, middle, _ = pieces(qall[s])
        qcat[s] = jnp.concatenate([high, high, middle], axis=0)
    for copy in sent:
        copy.wait_send()


def update_kernel(tile, merged, pcat, qcat, q_in, out_hbm, q_out, out, sems):
    tens, _, kt = qcat.shape
    copies = []
    for j in range(out.shape[0] // tile):
        here = slice(j * tile, (j + 1) * tile)
        basis = pcat[:, here].T
        for s in range(tens):
            outs = slice(s * kt, (s + 1) * kt)
            update = mm(basis, qcat[s], NN)
            out[here, outs] = (merged[here, outs] - update).astype(BF16)
        copy = pltpu.make_async_copy(out.at[here], out_hbm.at[here], sems.at[j])
        copy.start()
        copies.append(copy)
    q_out[...] = q_in[...]
    for copy in copies:
        copy.wait()


def solution(mesh):
    replicas, tens = mesh.shape["dp"], mesh.shape["tensor"]
    inner = 1
    while inner * inner < replicas or replicas % inner:
        inner += 1
    outer = replicas // inner

    def body(activations, cotangents, error_old, pause_positions, initial_q):
        rows, width = activations.shape
        kt = cotangents.shape[1]
        kw, rank = initial_q.shape
        mib = 1024 * 1024
        tile = math.gcd(width, 256)
        split = 2 * width // 5 // 128 * 128
        direct = replicas <= min(rank, 16)
        loads = 4 if width % 512 == 0 and rows % 64 == 0 else 1

        def reduce_bufs(span, n1, n2):
            h, cw = rank // n1, -(-span // (128 * n2)) * 128
            return [
                pltpu.VMEM((n1, h, cw * n2), F32),
                pltpu.VMEM((n1, h, cw * n2), F32),
                pltpu.VMEM((n2, h, cw), F32),
                pltpu.VMEM((n2, h, cw), F32),
                pltpu.VMEM((n1, n2, h, cw), F32),
            ]

        most = replicas if direct else max(inner, outer)
        hbm = pl.BlockSpec(memory_space=pltpu.HBM)
        vmem = pl.BlockSpec(memory_space=pltpu.VMEM)
        dma = pltpu.SemaphoreType.DMA
        merged, pcat, qcat, own_q = pl.pallas_call(
            functools.partial(kernel, (replicas, outer, inner, tens, split, direct)),
            out_shape=(
                pltpu.VMEM((width, kw), F32),
                pltpu.VMEM((3 * rank, width), BF16),
                pltpu.VMEM((tens, 3 * rank, kt), BF16),
                pltpu.VMEM((rank, kt), F32),
            ),
            in_specs=[hbm, hbm, hbm, vmem, vmem],
            out_specs=(vmem,) * 4,
            scratch_shapes=[
                pltpu.VMEM((rows, width), BF16),
                pltpu.VMEM((tens, rows, kt), BF16),
                pltpu.VMEM((width, kw), BF16),
                pltpu.VMEM((3 * rank, kw), BF16),
                pltpu.VMEM((width, rows), BF16),
                pltpu.VMEM((tens, rank, width), F32),
                pltpu.VMEM((tens, 3 * rank, width), BF16),
                pltpu.VMEM((tens, rank, kt), F32),
                pltpu.VMEM((tens, rank, kt), F32),
                pltpu.VMEM((tens, rank, kt), F32),
                *reduce_bufs(split, outer, inner),
                *reduce_bufs(width - split, inner, outer),
                *(reduce_bufs(kt, replicas, 1) if direct else reduce_bufs(kt, inner, outer)),
                dma((loads,)),
                dma((loads,)),
                dma((1,)),
                dma((4, tens)),
                dma((4, tens)),
                *[dma((4, most))] * 6,
            ],
            compiler_params=pltpu.CompilerParams(
                collective_id=0, has_side_effects=True, vmem_limit_bytes=36 * mib
            ),
            cost_estimate=pl.CostEstimate(
                flops=2 * rows * width * kw, bytes_accessed=2 * rows * width + 4 * width * kw, transcendentals=0
            ),
        )(*(
            pltpu.with_memory_space_constraint(x, pltpu.HBM)
            for x in (activations, cotangents, error_old, pause_positions, initial_q.T)
        ))
        error_new, q = pl.pallas_call(
            functools.partial(update_kernel, tile),
            out_shape=(
                jax.ShapeDtypeStruct(error_old.shape, BF16),
                jax.ShapeDtypeStruct((rank, kt), F32),
            ),
            in_specs=[vmem] * 4,
            out_specs=(hbm, vmem),
            scratch_shapes=[pltpu.VMEM((width, kw), BF16), dma((width // tile,))],
            compiler_params=pltpu.CompilerParams(vmem_limit_bytes=16 * mib),
        )(merged, pcat, qcat, own_q)
        return error_new, q.T

    return jax.shard_map(
        body,
        mesh=mesh,
        in_specs=(P("dp", "tensor"), P("dp", "tensor"), P(("dp", "tensor"), None), P(), P()),
        out_specs=(P(("dp", "tensor"), None), P("tensor", None)),
        check_vma=False,
    )
```
